32 devices in a mesh: ha: 4 (over z), wa: 8 (over y, x, core).
Axes of the slice: x: 2, y: 2, z: 4, core: 2. Of those that a mesh axis runs over, the one named last changes fastest.
Arguments:
- features: bfloat16 [128, 256, 256], P('ha', 'wa'), may hold values from -6 to 6
- counts: int32 [4, 8], P('ha', 'wa'), may hold values from 0 to 16, as said below
- owner_perm: int32 [4, 8], P('ha'), may hold values from 0 to 7, each once within a row
- corners: int32 [512, 2], P(('ha', 'wa')), may hold values from 0 to 31, as said below
- offsets: int32 [512, 28], P(('ha', 'wa')), may hold values from 0 to 124
- kernels: bfloat16 [2, 3, 3, 256, 256], replicated, may hold values from -0.125 to 0.125
- cotangent: bfloat16 [256, 14, 14, 256], P(('ha', 'wa')), may hold values from -6 to 6
Outputs:
- grad_features: float32 [128, 256, 256], P('ha', 'wa')
- grad_kernels: float32 [2, 3, 3, 256, 256], replicated
The draws below stay inside these ranges and needn't reach their ends.
Inputs may be any that keep to these rules, and one draw needn't show every extreme that they name: In each row of tiles the counts add up to 8 times the number of devices along wa, and one tile of every row has exactly 16. `corners`: the first column is below 32, the second below 32.
All inputs are finite; a program needn't handle non-finite values.
Results may differ from the reference program's by a relative error of at most 0.012.
Values may be sent and summed in bfloat16 or wider, within the bound.
A program may use at most 192 MiB of HBM per device.

```python
import jax
import jax.numpy as jnp
from jax import lax

TH = 32
TW = 32
C = 256
SIDE = 14
BOX = 32
LAYERS = 2
REG_DEV = 8
TILE_REGION_MAX = 16
H = 128
W = 256
REG = 256
SLOTS = 512
N_HA = 4
N_WA = 8


def draw_counts(key, part):

    def one_row(random_row_key):
        selection_key, extra_priority_key, ranking_key = jax.random.split(random_row_key, 3)
        chosen = jax.random.randint(selection_key, (), 0, N_WA)
        extra_priority = jax.random.randint(extra_priority_key, (N_WA,), 0, 2)
        region_ranking = jax.random.permutation(ranking_key, N_WA * TILE_REGION_MAX).astype(jnp.int32)
        owning_tile = jnp.arange(N_WA * TILE_REGION_MAX, dtype=jnp.int32) // TILE_REGION_MAX
        region_score = extra_priority[owning_tile] * (N_WA * TILE_REGION_MAX) + region_ranking
        region_score = jnp.where(owning_tile == chosen, -1 - region_ranking, region_score)
        ignored, picked = lax.top_k(region_score, REG_DEV * N_WA - TILE_REGION_MAX)
        taken = jnp.sum((owning_tile[picked][:, None] == jnp.arange(N_WA, dtype=jnp.int32)[None, :]).astype(jnp.int32), axis=0)
        return (taken + TILE_REGION_MAX * (jnp.arange(N_WA, dtype=jnp.int32) == chosen).astype(jnp.int32)).astype(jnp.int32)
    row_keys = jax.random.split(jax.random.fold_in(key, 7), N_HA)
    return jax.vmap(one_row)(row_keys)


def draw_corners(key, part):
    random_row_key, col_key = jax.random.split(jax.random.fold_in(key, 11))
    top_rows = jax.random.randint(random_row_key, (N_HA * N_WA * TILE_REGION_MAX, 1), 0, TH)
    left_cols = jax.random.randint(col_key, (N_HA * N_WA * TILE_REGION_MAX, 1), 0, TW)
    return jnp.concatenate([top_rows, left_cols], axis=1).astype(jnp.int32)


def plant(values, key, low, largest):
    longest = values.shape.index(max(values.shape))
    spots = []
    for shift in (0, 1):
        where = [jax.random.randint(jax.random.fold_in(key, axis), (), 0, length) for axis, length in enumerate(values.shape)]
        where[longest] = (where[longest] + shift) % values.shape[longest]
        spots.append(tuple(where))
    return values.at[spots[0]].set(low).at[spots[1]].set(largest)


def steps_of(own_key, shape, pieces, least, top_value):
    level = 1.0
    for position, shards_of in pieces:
        steps = jax.random.uniform(jax.random.fold_in(jax.random.fold_in(own_key, 6), position), (shards_of,), jnp.float32, least / len(pieces), top_value / len(pieces))
        level = level * jnp.repeat(jnp.exp(steps), shape[position] // shards_of).reshape((-1,) + (1,) * (len(shape) - 1 - position))
    return level


def normal_values(own_key, extent, scale, bound, cuts=(), kind=jnp.bfloat16):
    values = scale * jax.random.normal(own_key, extent, jnp.float32)
    if cuts:
        values = values * steps_of(own_key, extent, cuts, -0.22, 0.18)
    return jnp.clip(values, -bound, bound).astype(kind)


def setup_inputs(seed: int = 0) -> dict:
    key_list = jax.random.split(jax.random.key(seed), 8)
    features = normal_values(key_list[0], (H, W, C), 1.0, 6.0, ((0, 4), (1, 8)))
    counts = draw_counts(jax.random.fold_in(key_list[7], 71), 0)
    owner_perm = jax.vmap(lambda own: jax.random.permutation(own, N_WA))(jax.random.split(key_list[2], N_HA)).reshape((N_HA, N_WA)).astype(jnp.int32)
    corners = draw_corners(jax.random.fold_in(key_list[7], 71), 0)
    offsets = plant(jax.random.randint(key_list[4], (SLOTS, 2 * SIDE), 0, 4 * BOX - 3), jax.random.fold_in(key_list[4], 1), 0, (4 * BOX - 3) - 1).astype(jnp.int32)
    kernels = normal_values(key_list[5], (LAYERS, 3, 3, C, C), (9 * C) ** -0.5, 0.125)
    cotangent = normal_values(key_list[6], (REG, SIDE, SIDE, C), 1.0, 6.0, ((0, 32),))
    return dict(features=features, counts=counts, owner_perm=owner_perm, corners=corners, offsets=offsets, kernels=kernels, cotangent=cotangent)


highest = lax.Precision.HIGHEST

def tent_weights(sample_offsets):
    places = 4 * jnp.arange(BOX, dtype=jnp.int32)
    spread = jnp.abs(places[None, :] - sample_offsets[..., :, None]).astype(jnp.float32)
    return jnp.maximum(0.0, 1.0 - spread / 4.0)

def convolve(inputs, kernel):
    return lax.conv_general_dilated(inputs, kernel, (1, 1), 'SAME', dimension_numbers=('NHWC', 'HWIO', 'NHWC'), precision=highest)

def gelu_exact(values):
    return jax.nn.gelu(values, approximate=False)

def reference(features, counts, owner_perm, corners, offsets, kernels, cotangent):
    row_tiles, col_tiles = counts.shape
    slot_total = corners.shape[0]
    capacity = slot_total // (row_tiles * col_tiles)
    regions = cotangent.shape[0]
    channels = features.shape[2]
    height, breadth = (features.shape[0], features.shape[1])
    slot_ids = jnp.arange(slot_total, dtype=jnp.int32)
    tile_ids = slot_ids // capacity
    within = slot_ids % capacity
    tile_row = tile_ids // col_tiles
    tile_col = tile_ids % col_tiles
    starts = (jnp.cumsum(counts, axis=1) - counts).astype(jnp.int32)
    live_slot = within < counts[tile_row, tile_col]
    stream = (starts[tile_row, tile_col] + within).astype(jnp.int32)
    owner_slot = (tile_row * col_tiles + owner_perm[tile_row, stream % col_tiles]) * REG_DEV + stream // col_tiles
    target = jnp.where(live_slot, owner_slot, regions).astype(jnp.int32)
    source = jnp.zeros((regions,), jnp.int32).at[target].set(slot_ids, mode='drop')
    top_rows = (tile_row * TH + corners[:, 0]).astype(jnp.int32)
    left_cols = (tile_col * TW + corners[:, 1]).astype(jnp.int32)
    padded = jnp.pad(features, ((0, BOX), (0, BOX), (0, 0)))

    def block_step(running, region_ids):
        grad_map, kernel_sum = running
        chosen = source[region_ids]
        block_tops = top_rows[chosen]
        block_lefts = left_cols[chosen]
        windows = jax.vmap(lambda top_row, left_col: lax.dynamic_slice(padded, (top_row, left_col, jnp.int32(0)), (BOX, BOX, channels)))(block_tops, block_lefts)
        row_weights = tent_weights(offsets[chosen, :SIDE])
        col_weights = tent_weights(offsets[chosen, SIDE:])
        partial_rows = jnp.einsum('nip,npqc->niqc', row_weights, windows.astype(jnp.float32), precision=highest)
        samples = jnp.einsum('njq,niqc->nijc', col_weights, partial_rows, precision=highest).astype(jnp.bfloat16)
        inputs = [samples]
        before = []
        for layer_step in range(LAYERS):
            values = convolve(inputs[layer_step].astype(jnp.float32), kernels[layer_step].astype(jnp.float32))
            before.append(values)
            inputs.append(gelu_exact(values).astype(jnp.bfloat16))
        upward = cotangent[region_ids]
        layer_grads = [None] * LAYERS
        for layer_step in reversed(range(LAYERS)):
            ignored, gelu_slope = jax.vjp(gelu_exact, before[layer_step])
            inner_grad = gelu_slope(upward.astype(jnp.float32))[0].astype(jnp.bfloat16)
            ignored, pullback = jax.vjp(convolve, inputs[layer_step].astype(jnp.float32), kernels[layer_step].astype(jnp.float32))
            input_grad, kernel_grad = pullback(inner_grad.astype(jnp.float32))
            layer_grads[layer_step] = kernel_grad
            upward = input_grad.astype(jnp.bfloat16)
        spread_cols = jnp.einsum('njq,nijc->niqc', col_weights, upward.astype(jnp.float32), precision=highest)
        window_grads = jnp.einsum('nip,niqc->npqc', row_weights, spread_cols, precision=highest)
        for member in range(region_ids.shape[0]):
            corner_at = (block_tops[member], block_lefts[member], jnp.int32(0))
            current = lax.dynamic_slice(grad_map, corner_at, (BOX, BOX, channels))
            grad_map = lax.dynamic_update_slice(grad_map, current + window_grads[member], corner_at)
        return ((grad_map, kernel_sum + jnp.stack(layer_grads)), None)
    blocks = jnp.arange(regions, dtype=jnp.int32).reshape(regions // 8, 8)
    start_map = jnp.zeros((height + BOX, breadth + BOX, channels), jnp.float32)
    start_sum = jnp.zeros((LAYERS, 3, 3, channels, channels), jnp.float32)
    (grad_map, kernel_sum), ignored = lax.scan(block_step, (start_map, start_sum), blocks)
    return (grad_map[:height, :breadth], kernel_sum)
```

```python
import jax
import jax.numpy as jnp
from jax import lax
from jax.experimental import pallas as pl
from jax.experimental.pallas import tpu as pltpu
from jax.sharding import PartitionSpec as P

SIDE = 14
BOX = 32
LAYERS = 2
GRID = 16
CELLS = GRID * GRID
FAR = 4096.0
VMEM_BYTES = 56 * 2**20


def shifted(value, steps_ha, steps_wa):
    rows, cols = lax.axis_size("ha"), lax.axis_size("wa")
    pairs = []
    for row in range(rows):
        for col in range(cols):
            to_row, to_col = row + steps_ha, col + steps_wa
            if 0 <= to_row < rows and 0 <= to_col < cols:
                pairs.append((row * cols + col, to_row * cols + to_col))
    return lax.ppermute(value, ("ha", "wa"), pairs)


def gelu_and_slope(v):
    phi = 0.5 * (1.0 + lax.erf(v * 0.7071067811865476))
    slope = phi + v * (0.3989422804014327 * jnp.exp(-0.5 * v * v))
    return v * phi, slope


def cell_mask(rows, channels):
    at = lax.broadcasted_iota(jnp.int32, (rows, channels), 0)
    return jnp.logical_and(at % GRID < SIDE, (at // GRID) % GRID < SIDE)


def fill_shifts(ref, value, sign):
    rows, channels = value.shape
    zero = jnp.zeros((GRID, 3 * channels), jnp.bfloat16)
    ref[0:GRID, :] = zero
    ref[GRID + rows : 2 * GRID + rows, :] = zero
    for d in range(3):
        steps = (-sign * (d - 1)) % rows
        moved = pltpu.roll(value, steps, 0) if steps else value
        ref[GRID : GRID + rows, d * channels : (d + 1) * channels] = moved.astype(jnp.bfloat16)


def forward_kernel(
    tops, ext_ref, row_ref, col_ref, w_ref, x0t_ref, x1t_ref, s0_ref, s1_ref, mix, stack, value
):
    group = row_ref.shape[0] // CELLS
    rows = group * CELLS
    span, channels = ext_ref.shape[1], ext_ref.shape[2]
    step = pl.program_id(0)
    lane = lax.broadcasted_iota(jnp.int32, (CELLS, 2 * span), 1)
    upper = (lane >= span).astype(jnp.float32)
    across = (lane % span).astype(jnp.float32)
    for s in range(group):
        here = slice(s * CELLS, (s + 1) * CELLS)
        reach = jnp.maximum(0.0, 1.0 - jnp.abs(across - col_ref[here, :]))
        away = upper - row_ref[here, :]
        for k in range(BOX // 2):
            weight = jnp.maximum(0.0, 1.0 - jnp.abs(away + float(2 * k)))
            mix[:, k * 2 * span : (k + 1) * 2 * span] = (weight * reach).astype(jnp.bfloat16)
        top = tops[step * group + s]
        window = ext_ref[pl.ds(top, BOX)].reshape(BOX * span, channels)
        value[here, :] = jnp.dot(mix[...], window, preferred_element_type=jnp.float32)
    keep = cell_mask(rows, channels)

    def conv(layer):
        total = jnp.dot(stack[0:rows, :], w_ref[layer, 0], preferred_element_type=jnp.float32)
        for dy in range(1, 3):
            total += jnp.dot(
                stack[dy * GRID : dy * GRID + rows, :],
                w_ref[layer, dy],
                preferred_element_type=jnp.float32,
            )
        return total

    samples = value[...]
    x0t_ref[...] = samples.T.astype(jnp.bfloat16)
    fill_shifts(stack, samples, 1)
    act, slope = gelu_and_slope(conv(0))
    s0_ref[...] = jnp.where(keep, slope, 0.0)
    act = jnp.where(keep, act, 0.0)
    x1t_ref[...] = act.T.astype(jnp.bfloat16)
    fill_shifts(stack, act, 1)
    _, slope = gelu_and_slope(conv(1))
    s1_ref[...] = slope


def add_kernel_grads(g_ref, xt_ref, stack):
    rows = xt_ref.shape[1]
    channels = xt_ref.shape[0]

    @pl.when(pl.program_id(0) == 0)
    def _():
        g_ref[...] = jnp.zeros_like(g_ref)

    xt = xt_ref[...]
    for dy in range(3):
        for dx in range(3):
            g_ref[dy, dx] += jnp.dot(
                xt,
                stack[2 * GRID - dy * GRID : 2 * GRID - dy * GRID + rows, dx * channels : (dx + 1) * channels],
                preferred_element_type=jnp.float32,
            )


def back_through(wt_ref, stack, rows):
    total = jnp.dot(stack[2 * GRID : 2 * GRID + rows, :], wt_ref[0], preferred_element_type=jnp.float32)
    for dy in range(1, 3):
        total += jnp.dot(
            stack[2 * GRID - dy * GRID : 2 * GRID - dy * GRID + rows, :],
            wt_ref[dy],
            preferred_element_type=jnp.float32,
        )
    return total


def top_layer_kernel(route, inc_ref, s1_ref, s0_ref, x1t_ref, wt_ref, g_ref, pg_ref, stack, value):
    rows, channels = s1_ref.shape
    group = rows // CELLS
    used = inc_ref.shape[1]
    step = pl.program_id(0)
    for s in range(group):
        slot = step * group + s
        live = route[1, slot].astype(jnp.float32)
        value[s * CELLS : s * CELLS + used, :] = inc_ref[route[0, slot]].astype(jnp.float32) * live
        value[s * CELLS + used : (s + 1) * CELLS, :] = jnp.zeros((CELLS - used, channels), jnp.float32)
    fill_shifts(stack, value[...] * s1_ref[...], -1)
    add_kernel_grads(g_ref, x1t_ref, stack)
    grad = back_through(wt_ref, stack, rows)
    pg_ref[...] = (grad.astype(jnp.bfloat16).astype(jnp.float32) * s0_ref[...]).astype(jnp.bfloat16)


def low_grads_kernel(pg_ref, x0t_ref, g_ref, stack):
    fill_shifts(stack, pg_ref[...].astype(jnp.float32), -1)
    add_kernel_grads(g_ref, x0t_ref, stack)


def spread_kernel(tops, pg_ref, place_ref, wt_ref, out_ref, stack, value):
    rows, channels = pg_ref.shape
    group = rows // CELLS
    span = out_ref.shape[1]
    part = 8
    step = pl.program_id(0)

    @pl.when(step == 0)
    def _():
        out_ref[...] = jnp.zeros_like(out_ref)

    fill_shifts(stack, pg_ref[...].astype(jnp.float32), -1)
    value[...] = back_through(wt_ref, stack, rows).astype(jnp.bfloat16)
    across = lax.broadcasted_iota(jnp.int32, (span, CELLS), 0).astype(jnp.float32)
    for s in range(group):
        row_at = place_ref[s, 0:1, :]
        col_at = place_ref[s, 1:2, :]
        reach = jnp.maximum(0.0, 1.0 - jnp.abs(across - col_at))
        grad = value[s * CELLS : (s + 1) * CELLS, :]
        top = tops[step * group + s]
        for k in range(BOX // part):
            pieces = []
            for p in range(part):
                weight = jnp.maximum(0.0, 1.0 - jnp.abs(float(k * part + p) - row_at))
                pieces.append((weight * reach).astype(jnp.bfloat16))
            mixed = jnp.concatenate(pieces, axis=0)
            spread = jnp.dot(mixed, grad, preferred_element_type=jnp.float32)
            out_ref[pl.ds(top + k * part, part)] += spread.reshape(part, span, channels)


def pick_kernel(index, in_ref, out_ref):
    out_ref[...] = in_ref[...]


def params():
    return pltpu.CompilerParams(vmem_limit_bytes=VMEM_BYTES)


def cost(flops, nbytes, exps=0):
    return pl.CostEstimate(flops=flops, bytes_accessed=nbytes, transcendentals=exps)


def local(features, counts, owner_perm, corners, offsets, kernels, cotangent):
    tile_rows, tile_cols, channels = features.shape
    slot_total = corners.shape[0]
    owned = cotangent.shape[0]
    width_count = lax.axis_size("wa")
    pairs = slot_total // width_count
    col_index = lax.axis_index("wa")
    group = 4 if slot_total % 4 == 0 else 1
    steps = slot_total // group
    rows = group * CELLS
    all_rows = slot_total * CELLS
    span = tile_cols + BOX

    right_edge = shifted(features, 0, -1)
    lower_edge = shifted(features, -1, 0)
    corner_edge = shifted(features, -1, -1)

    row_counts = lax.all_gather(counts, "wa", axis=1, tiled=True)[0]
    starts = jnp.cumsum(row_counts) - row_counts
    device_ids = jnp.arange(width_count, dtype=jnp.int32)
    here_start = jnp.sum(jnp.where(device_ids == col_index, starts, 0))
    perm_row = owner_perm[0]
    slot_ids = jnp.arange(slot_total, dtype=jnp.int32)
    stream = here_start + slot_ids
    owner_of = jnp.sum(
        jnp.where((stream % width_count)[:, None] == device_ids[None, :], perm_row[None, :], 0),
        axis=1,
    )
    live_slot = (slot_ids < counts[0, 0]).astype(jnp.int32)
    route = jnp.stack([owner_of * pairs + slot_ids // width_count, live_slot])
    buffer_ids = jnp.arange(width_count * pairs, dtype=jnp.int32)
    position = jnp.sum(jnp.where(perm_row == col_index, device_ids, 0))
    sender_match = (buffer_ids // pairs)[:, None] == device_ids[None, :]
    sender_start = jnp.sum(jnp.where(sender_match, starts[None, :], 0), axis=1)
    arrival = (
        sender_start + (position - sender_start) % width_count + buffer_ids % pairs * width_count
    )
    chosen = jnp.clip(arrival // width_count, 0, owned - 1)
    padded = jnp.pad(cotangent, ((0, 0), (0, 0), (0, GRID - SIDE), (0, 0)))
    padded = padded.reshape(owned, SIDE * GRID, channels)
    block = (1, SIDE * GRID, channels)
    outgoing = pl.pallas_call(
        pick_kernel,
        out_shape=jax.ShapeDtypeStruct((width_count * pairs,) + block[1:], jnp.bfloat16),
        grid_spec=pltpu.PrefetchScalarGridSpec(
            num_scalar_prefetch=1,
            grid=(width_count * pairs,),
            in_specs=[pl.BlockSpec(block, lambda b, index: (index[b], 0, 0))],
            out_specs=pl.BlockSpec(block, lambda b, index: (b, 0, 0)),
        ),
    )(chosen, padded)
    incoming = lax.all_to_all(outgoing, "wa", split_axis=0, concat_axis=0, tiled=True)

    fill = ((0, 0), (0, GRID - SIDE))
    row_at = jnp.pad(offsets[:, :SIDE].astype(jnp.float32) * 0.25, fill, constant_values=FAR)
    col_at = offsets[:, SIDE:].astype(jnp.float32) * 0.25 + corners[:, 1:2].astype(jnp.float32)
    col_at = jnp.pad(col_at, fill, constant_values=FAR)
    row_cell = jnp.broadcast_to(row_at[:, :, None], (slot_total, GRID, GRID)).reshape(slot_total, CELLS)
    col_cell = jnp.broadcast_to(col_at[:, None, :], (slot_total, GRID, GRID)).reshape(slot_total, CELLS)
    place = jnp.stack([row_cell, col_cell], axis=1)
    row_wide = jnp.broadcast_to(row_cell.reshape(all_rows, 1), (all_rows, 2 * span))
    col_wide = jnp.broadcast_to(col_cell.reshape(all_rows, 1), (all_rows, 2 * span))
    tops = corners[:, 0]

    extended = jnp.concatenate(
        [
            jnp.concatenate([features, right_edge], axis=1),
            jnp.concatenate([lower_edge, corner_edge], axis=1),
        ],
        axis=0,
    )
    ahead = kernels.reshape(LAYERS, 3, 3 * channels, channels)
    back = kernels.transpose(0, 1, 2, 4, 3).reshape(LAYERS, 3, 3 * channels, channels)
    conv_flops = 2 * all_rows * 9 * channels * channels

    def tall(width):
        return pl.BlockSpec((rows, width), lambda t, *_: (t, 0))

    def wide():
        return pl.BlockSpec((channels, rows), lambda t, *_: (0, t))

    def fixed(shape):
        return pl.BlockSpec(shape, lambda t, *_: (0,) * len(shape))

    f32 = lambda *shape: jax.ShapeDtypeStruct(shape, jnp.float32)
    b16 = lambda *shape: jax.ShapeDtypeStruct(shape, jnp.bfloat16)
    stack_scratch = pltpu.VMEM((rows + 2 * GRID, 3 * channels), jnp.bfloat16)
    value_scratch = pltpu.VMEM((rows, channels), jnp.float32)
    grads_shape = (3, 3, channels, channels)

    x0t, x1t, slope0, slope1 = pl.pallas_call(
        forward_kernel,
        out_shape=(
            b16(channels, all_rows),
            b16(channels, all_rows),
            f32(all_rows, channels),
            f32(all_rows, channels),
        ),
        grid_spec=pltpu.PrefetchScalarGridSpec(
            num_scalar_prefetch=1,
            grid=(steps,),
            in_specs=[fixed(extended.shape), tall(2 * span), tall(2 * span), fixed(ahead.shape)],
            out_specs=(wide(), wide(), tall(channels), tall(channels)),
            scratch_shapes=[
                pltpu.VMEM((CELLS, BOX * span), jnp.bfloat16),
                stack_scratch,
                value_scratch,
            ],
        ),
        compiler_params=params(),
        cost_estimate=cost(2 * conv_flops + 2 * all_rows * BOX * span * channels, 24 * 2**20, 4 * all_rows * channels),
    )(tops, extended, row_wide, col_wide, ahead)

    top_grads, pre_grad = pl.pallas_call(
        top_layer_kernel,
        out_shape=(f32(*grads_shape), b16(all_rows, channels)),
        grid_spec=pltpu.PrefetchScalarGridSpec(
            num_scalar_prefetch=1,
            grid=(steps,),
            in_specs=[
                fixed(incoming.shape),
                tall(channels),
                tall(channels),
                wide(),
                fixed((3, 3 * channels, channels)),
            ],
            out_specs=(fixed(grads_shape), tall(channels)),
            scratch_shapes=[stack_scratch, value_scratch],
        ),
        compiler_params=params(),
        cost_estimate=cost(2 * conv_flops, 16 * 2**20),
    )(route, incoming, slope1, slope0, x1t, back[1])
    top_total = lax.psum(top_grads.astype(jnp.bfloat16), ("ha", "wa"))

    low_grads = pl.pallas_call(
        low_grads_kernel,
        out_shape=f32(*grads_shape),
        grid=(steps,),
        in_specs=[tall(channels), wide()],
        out_specs=fixed(grads_shape),
        scratch_shapes=[stack_scratch],
        compiler_params=params(),
        cost_estimate=cost(conv_flops, 8 * 2**20),
    )(pre_grad, x0t)
    low_total = lax.psum(low_grads.astype(jnp.bfloat16), ("ha", "wa"))

    grads_ext = pl.pallas_call(
        spread_kernel,
        out_shape=f32(tile_rows + BOX, span, channels),
        grid_spec=pltpu.PrefetchScalarGridSpec(
            num_scalar_prefetch=1,
            grid=(steps,),
            in_specs=[
                tall(channels),
                pl.BlockSpec((group, 2, CELLS), lambda t, *_: (t, 0, 0)),
                fixed((3, 3 * channels, channels)),
            ],
            out_specs=fixed((tile_rows + BOX, span, channels)),
            scratch_shapes=[stack_scratch, pltpu.VMEM((rows, channels), jnp.bfloat16)],
        ),
        compiler_params=params(),
        cost_estimate=cost(conv_flops + 2 * all_rows * BOX * span * channels, 8 * 2**20),
    )(tops, pre_grad, place, back[0])
    to_right = grads_ext[:tile_rows, tile_cols:].astype(jnp.bfloat16)
    to_below = grads_ext[tile_rows:, :tile_cols].astype(jnp.bfloat16)
    to_corner = grads_ext[tile_rows:, tile_cols:].astype(jnp.bfloat16)
    from_left = shifted(to_right, 0, 1).astype(jnp.float32)
    from_above = shifted(to_below, 1, 0).astype(jnp.float32)
    from_corner = shifted(to_corner, 1, 1).astype(jnp.float32)
    grad_tile = grads_ext[:tile_rows, :tile_cols]
    grad_tile = grad_tile.at[:, :BOX].add(from_left)
    grad_tile = grad_tile.at[:BOX].add(from_above)
    grad_tile = grad_tile.at[:BOX, :BOX].add(from_corner)
    kernel_grads = jnp.stack([low_total, top_total]).astype(jnp.float32)
    return (grad_tile, kernel_grads)


def solution(mesh):
    in_specs = (
        P("ha", "wa", None),
        P("ha", "wa"),
        P("ha", None),
        P(("ha", "wa"), None),
        P(("ha", "wa"), None),
        P(),
        P(("ha", "wa"), None, None, None),
    )
    out_specs = (P("ha", "wa", None), P())
    return jax.shard_map(local, mesh=mesh, in_specs=in_specs, out_specs=out_specs, check_vma=False)
```

```python
import jax
import jax.numpy as jnp
from jax import lax
from jax.experimental import pallas as pl
from jax.experimental.pallas import tpu as pltpu
from jax.sharding import PartitionSpec as P

SIDE = 14
BOX = 32
LAYERS = 2
GRID = 16
CELLS = GRID * GRID
FAR = 4096.0
VMEM_BYTES = 56 * 2**20


def shifted(value, steps_ha, steps_wa):
    rows, cols = lax.axis_size("ha"), lax.axis_size("wa")
    pairs = []
    for row in range(rows):
        for col in range(cols):
            to_row, to_col = row + steps_ha, col + steps_wa
            if 0 <= to_row < rows and 0 <= to_col < cols:
                pairs.append((row * cols + col, to_row * cols + to_col))
    return lax.ppermute(value, ("ha", "wa"), pairs)


def gelu_and_slope(v):
    phi = 0.5 * (1.0 + lax.erf(v * 0.7071067811865476))
    slope = phi + v * (0.3989422804014327 * jnp.exp(-0.5 * v * v))
    return v * phi, slope


def cell_mask(rows, channels):
    at = lax.broadcasted_iota(jnp.int32, (rows, channels), 0)
    return jnp.logical_and(at % GRID < SIDE, (at // GRID) % GRID < SIDE)


def fill_shifts(ref, value, sign):
    rows, channels = value.shape
    zero = jnp.zeros((GRID, 3 * channels), jnp.bfloat16)
    ref[0:GRID, :] = zero
    ref[GRID + rows : 2 * GRID + rows, :] = zero
    for d in range(3):
        steps = (-sign * (d - 1)) % rows
        moved = pltpu.roll(value, steps, 0) if steps else value
        ref[GRID : GRID + rows, d * channels : (d + 1) * channels] = moved.astype(jnp.bfloat16)


def forward_kernel(
    tops, ext_ref, row_ref, col_ref, w_ref, x0t_ref, x1t_ref, s0_ref, s1_ref, mix, stack, value
):
    group = row_ref.shape[0] // CELLS
    rows = group * CELLS
    span, channels = ext_ref.shape[1], ext_ref.shape[2]
    step = pl.program_id(0)
    lane = lax.broadcasted_iota(jnp.int32, (CELLS, 2 * span), 1)
    upper = (lane >= span).astype(jnp.float32)
    across = (lane % span).astype(jnp.float32)
    for s in range(group):
        here = slice(s * CELLS, (s + 1) * CELLS)
        reach = jnp.maximum(0.0, 1.0 - jnp.abs(across - col_ref[here, :]))
        away = upper - row_ref[here, :]
        for k in range(BOX // 2):
            weight = jnp.maximum(0.0, 1.0 - jnp.abs(away + float(2 * k)))
            mix[:, k * 2 * span : (k + 1) * 2 * span] = (weight * reach).astype(jnp.bfloat16)
        top = tops[step * group + s]
        window = ext_ref[pl.ds(top, BOX)].reshape(BOX * span, channels)
        value[here, :] = jnp.dot(mix[...], window, preferred_element_type=jnp.float32)
    keep = cell_mask(rows, channels)

    def conv(layer):
        total = jnp.dot(stack[0:rows, :], w_ref[layer, 0], preferred_element_type=jnp.float32)
        for dy in range(1, 3):
            total += jnp.dot(
                stack[dy * GRID : dy * GRID + rows, :],
                w_ref[layer, dy],
                preferred_element_type=jnp.float32,
            )
        return total

    samples = value[...]
    x0t_ref[...] = samples.T.astype(jnp.bfloat16)
    fill_shifts(stack, samples, 1)
    act, slope = gelu_and_slope(conv(0))
    s0_ref[...] = jnp.where(keep, slope, 0.0)
    act = jnp.where(keep, act, 0.0)
    x1t_ref[...] = act.T.astype(jnp.bfloat16)
    fill_shifts(stack, act, 1)
    _, slope = gelu_and_slope(conv(1))
    s1_ref[...] = slope


def add_kernel_grads(g_ref, xt_ref, stack):
    rows = xt_ref.shape[1]
    channels = xt_ref.shape[0]

    @pl.when(pl.program_id(0) == 0)
    def _():
        g_ref[...] = jnp.zeros_like(g_ref)

    xt = xt_ref[...]
    for dy in range(3):
        for dx in range(3):
            g_ref[dy, dx] += jnp.dot(
                xt,
                stack[2 * GRID - dy * GRID : 2 * GRID - dy * GRID + rows, dx * channels : (dx + 1) * channels],
                preferred_element_type=jnp.float32,
            )


def back_through(wt_ref, stack, rows):
    total = jnp.dot(stack[2 * GRID : 2 * GRID + rows, :], wt_ref[0], preferred_element_type=jnp.float32)
    for dy in range(1, 3):
        total += jnp.dot(
            stack[2 * GRID - dy * GRID : 2 * GRID - dy * GRID + rows, :],
            wt_ref[dy],
            preferred_element_type=jnp.float32,
        )
    return total


def top_layer_kernel(route, inc_ref, s1_ref, s0_ref, x1t_ref, wt_ref, g_ref, pg_ref, stack, value):
    rows, channels = s1_ref.shape
    group = rows // CELLS
    used = inc_ref.shape[1]
    step = pl.program_id(0)
    for s in range(group):
        slot = step * group + s
        live = route[1, slot].astype(jnp.float32)
        value[s * CELLS : s * CELLS + used, :] = inc_ref[route[0, slot]].astype(jnp.float32) * live
        value[s * CELLS + used : (s + 1) * CELLS, :] = jnp.zeros((CELLS - used, channels), jnp.float32)
    fill_shifts(stack, value[...] * s1_ref[...], -1)
    add_kernel_grads(g_ref, x1t_ref, stack)
    grad = back_through(wt_ref, stack, rows)
    pg_ref[...] = (grad.astype(jnp.bfloat16).astype(jnp.float32) * s0_ref[...]).astype(jnp.bfloat16)


def low_grads_kernel(pg_ref, x0t_ref, g_ref, stack):
    fill_shifts(stack, pg_ref[...].astype(jnp.float32), -1)
    add_kernel_grads(g_ref, x0t_ref, stack)


def spread_kernel(tops, pg_ref, place_ref, wt_ref, out_ref, stack, value):
    rows, channels = pg_ref.shape
    group = rows // CELLS
    span = out_ref.shape[1]
    part = 8
    step = pl.program_id(0)

    @pl.when(step == 0)
    def _():
        out_ref[...] = jnp.zeros_like(out_ref)

    fill_shifts(stack, pg_ref[...].astype(jnp.float32), -1)
    value[...] = back_through(wt_ref, stack, rows).astype(jnp.bfloat16)
    across = lax.broadcasted_iota(jnp.int32, (span, CELLS), 0).astype(jnp.float32)
    for s in range(group):
        row_at = place_ref[s, 0:1, :]
        col_at = place_ref[s, 1:2, :]
        reach = jnp.maximum(0.0, 1.0 - jnp.abs(across - col_at))
        grad = value[s * CELLS : (s + 1) * CELLS, :]
        top = tops[step * group + s]
        for k in range(BOX // part):
            pieces = []
            for p in range(part):
                weight = jnp.maximum(0.0, 1.0 - jnp.abs(float(k * part + p) - row_at))
                pieces.append((weight * reach).astype(jnp.bfloat16))
            mixed = jnp.concatenate(pieces, axis=0)
            spread = jnp.dot(mixed, grad, preferred_element_type=jnp.float32)
            out_ref[pl.ds(top + k * part, part)] += spread.reshape(part, span, channels)


def pick_kernel(index, in_ref, out_ref):
    out_ref[...] = in_ref[...]


def params():
    return pltpu.CompilerParams(vmem_limit_bytes=VMEM_BYTES)


def cost(flops, nbytes, exps=0):
    return pl.CostEstimate(flops=flops, bytes_accessed=nbytes, transcendentals=exps)


def local(features, counts, owner_perm, corners, offsets, kernels, cotangent):
    tile_rows, tile_cols, channels = features.shape
    slot_total = corners.shape[0]
    owned = cotangent.shape[0]
    width_count = lax.axis_size("wa")
    pairs = slot_total // width_count
    col_index = lax.axis_index("wa")
    group = 4 if slot_total % 4 == 0 else 1
    steps = slot_total // group
    rows = group * CELLS
    all_rows = slot_total * CELLS
    span = tile_cols + BOX

    right_edge = shifted(features, 0, -1)
    lower_edge = shifted(features, -1, 0)
    corner_edge = shifted(features, -1, -1)

    row_counts = lax.all_gather(counts, "wa", axis=1, tiled=True)[0]
    starts = jnp.cumsum(row_counts) - row_counts
    device_ids = jnp.arange(width_count, dtype=jnp.int32)
    here_start = jnp.sum(jnp.where(device_ids == col_index, starts, 0))
    perm_row = owner_perm[0]
    slot_ids = jnp.arange(slot_total, dtype=jnp.int32)
    stream = here_start + slot_ids
    owner_of = jnp.sum(
        jnp.where((stream % width_count)[:, None] == device_ids[None, :], perm_row[None, :], 0),
        axis=1,
    )
    live_slot = (slot_ids < counts[0, 0]).astype(jnp.int32)
    route = jnp.stack([owner_of * pairs + slot_ids // width_count, live_slot])
    buffer_ids = jnp.arange(width_count * pairs, dtype=jnp.int32)
    position = jnp.sum(jnp.where(perm_row == col_index, device_ids, 0))
    sender_match = (buffer_ids // pairs)[:, None] == device_ids[None, :]
    sender_start = jnp.sum(jnp.where(sender_match, starts[None, :], 0), axis=1)
    arrival = (
        sender_start + (position - sender_start) % width_count + buffer_ids % pairs * width_count
    )
    chosen = jnp.clip(arrival // width_count, 0, owned - 1)
    padded = jnp.pad(cotangent, ((0, 0), (0, 0), (0, GRID - SIDE), (0, 0)))
    padded = padded.reshape(owned, SIDE * GRID, channels)
    block = (1, SIDE * GRID, channels)
    outgoing = pl.pallas_call(
        pick_kernel,
        out_shape=jax.ShapeDtypeStruct((width_count * pairs,) + block[1:], jnp.bfloat16),
        grid_spec=pltpu.PrefetchScalarGridSpec(
            num_scalar_prefetch=1,
            grid=(width_count * pairs,),
            in_specs=[pl.BlockSpec(block, lambda b, index: (index[b], 0, 0))],
            out_specs=pl.BlockSpec(block, lambda b, index: (b, 0, 0)),
        ),
    )(chosen, padded)
    incoming = lax.all_to_all(outgoing, "wa", split_axis=0, concat_axis=0, tiled=True)

    fill = ((0, 0), (0, GRID - SIDE))
    row_at = jnp.pad(offsets[:, :SIDE].astype(jnp.float32) * 0.25, fill, constant_values=FAR)
    col_at = offsets[:, SIDE:].astype(jnp.float32) * 0.25 + corners[:, 1:2].astype(jnp.float32)
    col_at = jnp.pad(col_at, fill, constant_values=FAR)
    row_cell = jnp.broadcast_to(row_at[:, :, None], (slot_total, GRID, GRID)).reshape(slot_total, CELLS)
    col_cell = jnp.broadcast_to(col_at[:, None, :], (slot_total, GRID, GRID)).reshape(slot_total, CELLS)
    place = jnp.stack([row_cell, col_cell], axis=1)
    row_wide = jnp.broadcast_to(row_cell.reshape(all_rows, 1), (all_rows, 2 * span))
    col_wide = jnp.broadcast_to(col_cell.reshape(all_rows, 1), (all_rows, 2 * span))
    tops = corners[:, 0]

    extended = jnp.concatenate(
        [
            jnp.concatenate([features, right_edge], axis=1),
            jnp.concatenate([lower_edge, corner_edge], axis=1),
        ],
        axis=0,
    )
    ahead = kernels.reshape(LAYERS, 3, 3 * channels, channels)
    back = kernels.transpose(0, 1, 2, 4, 3).reshape(LAYERS, 3, 3 * channels, channels)
    conv_flops = 2 * all_rows * 9 * channels * channels

    def tall(width):
        return pl.BlockSpec((rows, width), lambda t, *_: (t, 0))

    def wide():
        return pl.BlockSpec((channels, rows), lambda t, *_: (0, t))

    def fixed(shape):
        return pl.BlockSpec(shape, lambda t, *_: (0,) * len(shape))

    f32 = lambda *shape: jax.ShapeDtypeStruct(shape, jnp.float32)
    b16 = lambda *shape: jax.ShapeDtypeStruct(shape, jnp.bfloat16)
    stack_scratch = pltpu.VMEM((rows + 2 * GRID, 3 * channels), jnp.bfloat16)
    value_scratch = pltpu.VMEM((rows, channels), jnp.float32)
    grads_shape = (3, 3, channels, channels)

    x0t, x1t, slope0, slope1 = pl.pallas_call(
        forward_kernel,
        out_shape=(
            b16(channels, all_rows),
            b16(channels, all_rows),
            f32(all_rows, channels),
            f32(all_rows, channels),
        ),
        grid_spec=pltpu.PrefetchScalarGridSpec(
            num_scalar_prefetch=1,
            grid=(steps,),
            in_specs=[fixed(extended.shape), tall(2 * span), tall(2 * span), fixed(ahead.shape)],
            out_specs=(wide(), wide(), tall(channels), tall(channels)),
            scratch_shapes=[
                pltpu.VMEM((CELLS, BOX * span), jnp.bfloat16),
                stack_scratch,
                value_scratch,
            ],
        ),
        compiler_params=params(),
        cost_estimate=cost(2 * conv_flops + 2 * all_rows * BOX * span * channels, 24 * 2**20, 4 * all_rows * channels),
    )(tops, extended, row_wide, col_wide, ahead)

    top_grads, pre_grad = pl.pallas_call(
        top_layer_kernel,
        out_shape=(f32(*grads_shape), b16(all_rows, channels)),
        grid_spec=pltpu.PrefetchScalarGridSpec(
            num_scalar_prefetch=1,
            grid=(steps,),
            in_specs=[
                fixed(incoming.shape),
                tall(channels),
                tall(channels),
                wide(),
                fixed((3, 3 * channels, channels)),
            ],
            out_specs=(fixed(grads_shape), tall(channels)),
            scratch_shapes=[stack_scratch, value_scratch],
        ),
        compiler_params=params(),
        cost_estimate=cost(2 * conv_flops, 16 * 2**20),
    )(route, incoming, slope1, slope0, x1t, back[1])

    low_grads = pl.pallas_call(
        low_grads_kernel,
        out_shape=f32(*grads_shape),
        grid=(steps,),
        in_specs=[tall(channels), wide()],
        out_specs=fixed(grads_shape),
        scratch_shapes=[stack_scratch],
        compiler_params=params(),
        cost_estimate=cost(conv_flops, 8 * 2**20),
    )(pre_grad, x0t)
    both = jnp.stack([low_grads, top_grads]).astype(jnp.bfloat16).reshape(-1, channels)
    share = lax.psum_scatter(both, "wa", scatter_dimension=0, tiled=True)
    share = lax.psum(share, "ha")
    total = lax.all_gather(share, "wa", axis=0, tiled=True)

    grads_ext = pl.pallas_call(
        spread_kernel,
        out_shape=f32(tile_rows + BOX, span, channels),
        grid_spec=pltpu.PrefetchScalarGridSpec(
            num_scalar_prefetch=1,
            grid=(steps,),
            in_specs=[
                tall(channels),
                pl.BlockSpec((group, 2, CELLS), lambda t, *_: (t, 0, 0)),
                fixed((3, 3 * channels, channels)),
            ],
            out_specs=fixed((tile_rows + BOX, span, channels)),
            scratch_shapes=[stack_scratch, pltpu.VMEM((rows, channels), jnp.bfloat16)],
        ),
        compiler_params=params(),
        cost_estimate=cost(conv_flops + 2 * all_rows * BOX * span * channels, 8 * 2**20),
    )(tops, pre_grad, place, back[0])
    to_right = grads_ext[:tile_rows, tile_cols:].astype(jnp.bfloat16)
    to_below = grads_ext[tile_rows:, :tile_cols].astype(jnp.bfloat16)
    to_corner = grads_ext[tile_rows:, tile_cols:].astype(jnp.bfloat16)
    from_left = shifted(to_right, 0, 1).astype(jnp.float32)
    from_above = shifted(to_below, 1, 0).astype(jnp.float32)
    from_corner = shifted(to_corner, 1, 1).astype(jnp.float32)
    grad_tile = grads_ext[:tile_rows, :tile_cols]
    grad_tile = grad_tile.at[:, :BOX].add(from_left)
    grad_tile = grad_tile.at[:BOX].add(from_above)
    grad_tile = grad_tile.at[:BOX, :BOX].add(from_corner)
    kernel_grads = total.astype(jnp.float32).reshape((LAYERS,) + grads_shape)
    return (grad_tile, kernel_grads)


def solution(mesh):
    in_specs = (
        P("ha", "wa", None),
        P("ha", "wa"),
        P("ha", None),
        P(("ha", "wa"), None),
        P(("ha", "wa"), None),
        P(),
        P(("ha", "wa"), None, None, None),
    )
    out_specs = (P("ha", "wa", None), P())
    return jax.shard_map(local, mesh=mesh, in_specs=in_specs, out_specs=out_specs, check_vma=False)
```
